512 devices in a mesh: fsdp: 32 (over x, z_lo, core), sp: 16 (over y, z_hi).
Axes of the slice: x: 4, y: 4, z: 16 (z_hi: 4, z_lo: 4; z = z_hi * 4 + z_lo), core: 2. Of those that a mesh axis runs over, the one named last changes fastest.
Arguments:
- query: bfloat16 [32, 2048, 4096], P('fsdp', 'sp'), may hold values from -6 to 6
- key: bfloat16 [32, 2048, 4096], P('fsdp', 'sp'), may hold values from -6 to 6
- value: bfloat16 [32, 2048, 4096], P('fsdp', 'sp'), may hold values from -6 to 6
- cotangent: bfloat16 [32, 2048, 4096], P('fsdp', 'sp')
- gain_q: float32 [32, 128], P('sp', 'fsdp'), may hold values from 0.5 to 5
- gain_k: float32 [32, 128], P('sp', 'fsdp'), may hold values from 0.5 to 5
- windows: int32 [16, 6], replicated, may hold values from 0 to 15, as said below
- order: int32 [2048], replicated, may hold values from 0 to 2047, as said below
Outputs:
- grad_gain_q: float32 [32, 128], P('sp', 'fsdp')
- grad_gain_k: float32 [32, 128], P('sp', 'fsdp')
The draws below stay inside these ranges and needn't reach their ends.
Inputs may be any that keep to these rules, and one draw needn't show every extreme that they name: `windows`: row t lists 6 different tiles, the first of them t itself. `order`: each of the 2048 positions appears once.
All inputs are finite; a program needn't handle non-finite values.
Results may differ from the reference program's by a relative error of at most 0.0035.
The reference program's roundings to bfloat16 on the way count: a program that leaves them out, or rounds other values in their place, can miss the bound.
Values may be sent and summed in bfloat16 or wider, within the bound.
No kernel may reach another device: no remote copies, remote signals or barrier semaphores. Data moves between devices by JAX's collectives and lax.ppermute only.
A program may use at most 64 MiB of HBM per device.

```python
import math
import jax
import jax.numpy as jnp
from jax import lax

HEAD_DIM = 128
TILE = 128
HEADS = 32
WIN = 2048
TILES = 16
NB = 6
CLIPS = 32


def tile_order(key):
    return jax.random.permutation(jax.random.fold_in(key, 101), WIN).astype(jnp.int32)


def draw_order(key, part):
    return tile_order(key)


def draw_query(key, part):
    own_key = jax.random.fold_in(key, 3)
    shape = (CLIPS, WIN, HEADS * HEAD_DIM)
    rows = jnp.clip(jax.random.normal(own_key, shape, jnp.float32), -6.0, 6.0)
    return rows.astype(jnp.bfloat16)


def draw_key(key, part):
    own_key = jax.random.fold_in(key, 5)
    shape = (CLIPS, WIN, HEADS * HEAD_DIM)
    rows = jnp.clip(jax.random.normal(own_key, shape, jnp.float32), -6.0, 6.0)
    return rows.astype(jnp.bfloat16)


def draw_gain_q(key, part):
    own_key = jax.random.fold_in(key, 13)
    spread = jnp.exp(jax.random.uniform(own_key, (HEADS, HEAD_DIM), jnp.float32, math.log(0.5), math.log(3.0)))
    return spread


def draw_gain_k(key, part):
    own_key = jax.random.fold_in(key, 17)
    spread = jnp.exp(jax.random.uniform(own_key, (HEADS, HEAD_DIM), jnp.float32, math.log(0.5), math.log(3.0)))
    return spread


def draw_cotangent(key, part):
    key = jax.random.fold_in(key, 7)
    shape = (CLIPS, WIN, HEADS * HEAD_DIM)
    steps = jnp.arange(CLIPS, dtype=jnp.float32) / max(CLIPS - 1, 1)
    rising = jnp.exp(jnp.log(3.0) * steps)
    base = jax.random.normal(key, shape, jnp.float32)
    return (base * rising[:, None, None] * float(CLIPS * WIN) ** (-0.5)).astype(jnp.bfloat16)


def draw_windows(key, part):
    key = jax.random.fold_in(key, 11)
    tiles = jnp.arange(TILES, dtype=jnp.int32)
    depth = tiles // 4
    row_pos = tiles // 2 % 2
    col_pos = tiles % 2
    distance = jnp.abs(depth[:, None] - depth[None, :]) + jnp.abs(row_pos[:, None] - row_pos[None, :]) + jnp.abs(col_pos[:, None] - col_pos[None, :])
    noise = jax.random.randint(key, (TILES, TILES), 0, 1024, jnp.int32)
    score = distance * 262144 + noise * 256 + tiles[None, :]
    unused, picked = lax.top_k(-score, NB)
    picked = picked.astype(jnp.int32)
    rest = picked[:, 1:]
    columns = jnp.arange(NB - 1, dtype=jnp.int32)
    shuffle = jax.random.randint(jax.random.fold_in(key, 1), (TILES, NB - 1), 0, 4096, jnp.int32) * NB + columns[None, :]
    places = jnp.argsort(shuffle, axis=1, stable=True)
    rest = jnp.take_along_axis(rest, places, axis=1)
    return jnp.concatenate([picked[:, :1], rest], axis=1).astype(jnp.int32)


def block_scale(stream_key, dims, cuts, low, largest):
    factor_of, own = 1.0, jax.random.fold_in(stream_key, 6)
    for position, parts in cuts:
        draws = jnp.exp(jax.random.uniform(jax.random.fold_in(own, position), (parts,), jnp.float32, low / len(cuts), largest / len(cuts)))
        factor_of = factor_of * jnp.repeat(draws, dims[position] // parts).reshape([-1 if axis == position else 1 for axis in range(len(dims))])
    return factor_of


def gaussian(key, dims, scale, most, shards=(), kind=jnp.bfloat16):
    result = scale * jax.random.normal(key, dims, jnp.float32)
    if shards:
        result = result * block_scale(key, dims, shards, -0.22, 0.18)
    return jnp.clip(result, -most, most).astype(kind)


def setup_inputs(seed: int = 0) -> dict:
    seeds = jax.random.split(jax.random.key(seed), 9)
    return {
        "query": draw_query(jax.random.fold_in(seeds[8], 71), 0),
        "key": draw_key(jax.random.fold_in(seeds[8], 71), 0),
        "value": gaussian(seeds[2], (CLIPS, WIN, HEADS * HEAD_DIM), 1.0, 6.0, ((0, 32), (1, 16))),
        "cotangent": draw_cotangent(jax.random.fold_in(seeds[8], 71), 0),
        "gain_q": draw_gain_q(jax.random.fold_in(seeds[8], 71), 0),
        "gain_k": draw_gain_k(jax.random.fold_in(seeds[8], 71), 0),
        "windows": draw_windows(jax.random.fold_in(seeds[8], 71), 0),
        "order": draw_order(jax.random.fold_in(seeds[8], 71), 0),
    }


def normalize(rows, gain):
    wide = rows.astype(jnp.float32)
    unit = wide * lax.rsqrt(lax.optimization_barrier(jnp.mean(wide * wide, axis=-1, keepdims=True)) + 1e-06)
    return (unit, (unit * gain).astype(jnp.bfloat16))

def attend_forward(query_rows, key_rows, value_rows, gain_query, gain_key, windows):
    tiles, tile, width = query_rows.shape
    count = windows.shape[1]
    scale = width ** (-0.5)
    qhat, qnorm = normalize(query_rows, gain_query)
    khat, knorm = normalize(key_rows, gain_key)
    keys = knorm[windows].reshape(tiles, count * tile, width)
    values = value_rows[windows].reshape(tiles, count * tile, width)
    scores = jnp.einsum('tqd,tkd->tqk', qnorm, keys, preferred_element_type=jnp.float32) * scale
    top = lax.optimization_barrier(jnp.max(scores, axis=-1, keepdims=True))
    weights = jnp.exp(scores - top)
    probs = weights / lax.optimization_barrier(jnp.sum(weights, axis=-1, keepdims=True))
    attended = jnp.einsum('tqk,tkd->tqd', probs.astype(jnp.bfloat16), values, preferred_element_type=jnp.float32)
    return (qhat, khat, qnorm, keys, values, probs, attended)

def attend_backward(state, grad_rows, windows):
    qhat, khat, qnorm, keys, values, probs, attended = state
    tiles, tile, width = qhat.shape
    count = windows.shape[1]
    scale = width ** (-0.5)
    dprobs = jnp.einsum('tqd,tkd->tqk', grad_rows, values, preferred_element_type=jnp.float32)
    rowterm = lax.optimization_barrier(jnp.sum(grad_rows.astype(jnp.float32) * attended, axis=-1, keepdims=True))
    dscores = (probs * (dprobs - rowterm)).astype(jnp.bfloat16)
    dquery = jnp.einsum('tqk,tkd->tqd', dscores, keys, preferred_element_type=jnp.float32) * scale
    dkeys = jnp.einsum('tqk,tqd->tkd', dscores, qnorm, preferred_element_type=jnp.float32) * scale
    dkeys = dkeys.reshape(tiles, count, tile, width)
    onehot = (windows[:, :, None] == jnp.arange(tiles, dtype=jnp.int32)[None, None, :]).astype(jnp.float32)
    dkey_rows = jnp.einsum('tns,tnrd->srd', onehot, dkeys, precision=lax.Precision.HIGHEST)
    return (lax.optimization_barrier(jnp.sum(dquery * qhat, axis=(0, 1))), lax.optimization_barrier(jnp.sum(dkey_rows * khat, axis=(0, 1))))

def reference(query, key, value, cotangent, gain_q, gain_k, windows, order):

    def arrange(rows):
        rows = rows.reshape(WIN, HEADS, HEAD_DIM)[order]
        return jnp.transpose(rows.reshape(TILES, TILE, HEADS, HEAD_DIM), (2, 0, 1, 3))

    def per_head(items):
        query_rows, key_rows, value_rows, grad_rows, gain_query, gain_key = items
        state = attend_forward(query_rows, key_rows, value_rows, gain_query, gain_key, windows)
        return attend_backward(state, grad_rows, windows)

    def per_clip(carry, items):
        query_clip, key_clip, value_clip, grad_clip = items
        terms_q, terms_k = lax.map(per_head, (arrange(query_clip), arrange(key_clip), arrange(value_clip), arrange(grad_clip), gain_q, gain_k))
        return ((carry[0] + terms_q, carry[1] + terms_k), None)
    zeros = jnp.zeros((HEADS, HEAD_DIM), jnp.float32)
    totals, unused = lax.scan(per_clip, (zeros, zeros), (query, key, value, cotangent))
    return (totals[0], totals[1])
```

```python
import functools

import jax
import jax.numpy as jnp
from jax import lax
from jax.experimental import pallas as pl
from jax.experimental.pallas import tpu as pltpu
from jax.sharding import PartitionSpec as P

TILE = 128


def pack_kernel(head, heads, width, refs_in, out_ref, sems):
    copies = []
    for dest in range(out_ref.shape[0]):
        lanes = pl.ds((dest * heads + head) * width, width)
        for part, ref in enumerate(refs_in):
            copies.append(
                pltpu.make_async_copy(
                    ref.at[0, :, lanes],
                    out_ref.at[dest, :, pl.ds(part * width, width)],
                    sems.at[dest, part],
                )
            )
    for copy in copies:
        copy.start()
    for copy in copies:
        copy.wait()


def pack(arrays, head, heads, groups, width):
    tokens = arrays[0].shape[1]
    count = len(arrays)

    def body(*refs):
        pack_kernel(head, heads, width, refs[:count], refs[count], refs[count + 1])

    return pl.pallas_call(
        body,
        out_shape=jax.ShapeDtypeStruct((groups, tokens, count * width), jnp.bfloat16),
        in_specs=[pl.BlockSpec(memory_space=pl.ANY)] * count,
        out_specs=pl.BlockSpec(memory_space=pl.ANY),
        scratch_shapes=[pltpu.SemaphoreType.DMA((groups, count))],
        cost_estimate=pl.CostEstimate(
            flops=0, bytes_accessed=4 * groups * tokens * count * width, transcendentals=0
        ),
        name="pack_head",
    )(*arrays)


def head_kernel(
    head,
    win_ref,
    rows_ref,
    order_ref,
    gain_q_ref,
    gain_k_ref,
    out_ref,
    kv_ref,
    knt_ref,
    khat_ref,
    qhat_ref,
    qn_ref,
    qd_ref,
    accq_ref,
    acck_ref,
):
    tiles, count = win_ref.shape
    width = qn_ref.shape[-1]
    tokens = tiles * TILE
    scale = width ** (-0.5)
    gain_q = gain_q_ref[head : head + 1, :]
    gain_k = gain_k_ref[head : head + 1, :]
    qd_ref[...] = jnp.zeros_like(qd_ref)
    accq_ref[...] = jnp.zeros_like(accq_ref)
    acck_ref[...] = jnp.zeros_like(acck_ref)

    def unit_rows(rows):
        return rows * lax.rsqrt(jnp.mean(rows * rows, axis=-1, keepdims=True) + 1e-06)

    def arrange(step, carry):
        start = pl.multiple_of(step * 2 * TILE, 2 * TILE)
        places = order_ref[pl.ds(start, 2 * TILE), :]
        iota = lax.broadcasted_iota(jnp.int32, (2 * TILE, tokens), 1)
        onehot = jnp.where(places == iota, 1.0, 0.0).astype(jnp.bfloat16)
        picked = jnp.dot(onehot, rows_ref[...], preferred_element_type=jnp.float32)
        for half in range(2):
            tile = step * 2 + half
            part = picked[half * TILE : (half + 1) * TILE]
            qhat = unit_rows(part[:, :width])
            khat = unit_rows(part[:, width : 2 * width])
            qn = (qhat * gain_q).astype(jnp.bfloat16)
            kn = khat * gain_k
            kn16 = kn.astype(jnp.bfloat16)
            kv_ref[tile, :, :width] = kn16
            kv_ref[tile, :, width:] = part[:, 2 * width : 3 * width].astype(jnp.bfloat16)
            knt_ref[tile] = kn16.astype(jnp.float32).T.astype(jnp.bfloat16)
            khat_ref[tile] = khat
            qhat_ref[tile] = qhat.T
            qn_ref[tile] = qn
            qd_ref[tile, :TILE, :width] = qn
            qd_ref[tile, TILE:, width:] = part[:, 3 * width :].astype(jnp.bfloat16)
        return carry

    lax.fori_loop(0, tiles // 2, arrange, 0)

    def attend(tile, carry):
        picks = [win_ref[tile, n] for n in range(count)]
        keys_values = jnp.concatenate([kv_ref[pick] for pick in picks], axis=0)
        both = lax.dot_general(
            keys_values, qd_ref[tile], (((1,), (1,)), ((), ())), preferred_element_type=jnp.float32
        )
        scores, dprobs = both[:, :TILE], both[:, TILE:]
        top = jnp.max(scores, axis=0, keepdims=True)
        weights = jnp.exp((scores - top) * scale)
        inverse = 1.0 / jnp.sum(weights, axis=0, keepdims=True)
        probs = weights * inverse
        rounded = probs.astype(jnp.bfloat16).astype(jnp.float32)
        rowterm = jnp.sum(rounded * dprobs, axis=0, keepdims=True)
        dscores = (probs * (dprobs - rowterm)).astype(jnp.bfloat16)
        keys_t = jnp.concatenate([knt_ref[pick] for pick in picks], axis=1)
        dquery_t = jnp.dot(keys_t, dscores, preferred_element_type=jnp.float32)
        accq_ref[...] += dquery_t * qhat_ref[tile]
        dkeys = jnp.dot(dscores, qn_ref[tile], preferred_element_type=jnp.float32)
        total = dkeys[:TILE] * khat_ref[picks[0]]
        for n in range(1, count):
            total = total + dkeys[n * TILE : (n + 1) * TILE] * khat_ref[picks[n]]
        acck_ref[...] += total
        return carry

    lax.fori_loop(0, tiles, attend, 0)
    out_ref[0:1, :] = jnp.sum(accq_ref[...].T, axis=0, keepdims=True) * scale
    out_ref[1:2, :] = jnp.sum(acck_ref[...], axis=0, keepdims=True) * scale


def head_terms(rows, order_column, gain_q, gain_k, windows, head):
    tokens = rows.shape[0]
    tiles, count = windows.shape
    width = gain_q.shape[-1]
    vmem = pl.BlockSpec(memory_space=pltpu.VMEM)
    return pl.pallas_call(
        functools.partial(head_kernel, head),
        out_shape=jax.ShapeDtypeStruct((2, width), jnp.float32),
        in_specs=[pl.BlockSpec(memory_space=pltpu.SMEM), vmem, vmem, vmem, vmem],
        out_specs=vmem,
        scratch_shapes=[
            pltpu.VMEM((tiles, TILE, 2 * width), jnp.bfloat16),
            pltpu.VMEM((tiles, width, TILE), jnp.bfloat16),
            pltpu.VMEM((tiles, TILE, width), jnp.float32),
            pltpu.VMEM((tiles, width, TILE), jnp.float32),
            pltpu.VMEM((tiles, TILE, width), jnp.bfloat16),
            pltpu.VMEM((tiles, 2 * TILE, 2 * width), jnp.bfloat16),
            pltpu.VMEM((width, TILE), jnp.float32),
            pltpu.VMEM((TILE, width), jnp.float32),
        ],
        compiler_params=pltpu.CompilerParams(vmem_limit_bytes=40 * 2**20),
        cost_estimate=pl.CostEstimate(
            flops=2 * tokens * tokens * 4 * width + 10 * tokens * count * TILE * width,
            bytes_accessed=rows.size * 2,
            transcendentals=tokens * count * TILE,
        ),
        name="head_terms",
    )(windows, rows, order_column, gain_q, gain_k)


def shards(query, key, value, cotangent, gain_q, gain_k, windows, order):
    groups = lax.axis_size("sp")
    spread = lax.axis_size("fsdp")
    tokens = query.shape[1]
    flat = query.shape[2]
    heads = gain_q.shape[0]
    width = flat // (groups * heads)
    own = gain_q.shape[1]
    arrays = (query, key, value, cotangent)

    def exchange(packed):
        rows = lax.all_to_all(packed, "sp", split_axis=0, concat_axis=0, tiled=True)
        return rows.reshape(groups * tokens, len(arrays) * width)

    packed = [pack(arrays, head, heads, groups, width) for head in range(heads)]
    gains = lax.all_gather(jnp.stack([gain_q, gain_k]), "fsdp", axis=2, tiled=True)
    order_column = order.reshape(order.shape[0], 1)
    terms = []
    for head in range(heads):
        rows = exchange(packed[head])
        terms.append(head_terms(rows, order_column, gains[0], gains[1], windows, head))
    stacked = jnp.stack(terms).reshape(heads, 2, spread, own)
    stacked = jnp.transpose(stacked, (2, 1, 0, 3)).reshape(spread, 2 * heads * own)
    arrived = lax.all_to_all(stacked, "fsdp", split_axis=0, concat_axis=0, tiled=True)
    sums = jnp.sum(arrived, axis=0).reshape(2, heads, own)
    return (sums[0], sums[1])


def solution(mesh):
    placed = (
        P("fsdp", "sp", None),
        P("fsdp", "sp", None),
        P("fsdp", "sp", None),
        P("fsdp", "sp", None),
        P("sp", "fsdp"),
        P("sp", "fsdp"),
        P(),
        P(),
    )
    return jax.shard_map(
        shards,
        mesh=mesh,
        in_specs=placed,
        out_specs=(P("sp", "fsdp"), P("sp", "fsdp")),
        check_vma=False,
    )
```

```python
import jax
import jax.numpy as jnp
from jax import lax
from jax.experimental import pallas as pl
from jax.experimental.pallas import tpu as pltpu
from jax.sharding import PartitionSpec as P

TILE = 128
LOG2E = 1.4426950408889634
PARTS = 4


def pack(arrays, groups, heads, width):
    tokens, flat = arrays[0].shape[1:]
    rows = heads * PARTS
    chunks = 4
    span = flat // chunks

    def body(*refs):
        ins, out_ref = refs[:PARTS], refs[PARTS]
        held_ref, ready_ref, wide_ref, in_sems, out_sems = refs[PARTS + 1 :]
        arrivals = []
        for chunk in range(chunks):
            lanes = slice(chunk * span, (chunk + 1) * span)
            arrivals.append(
                [
                    pltpu.make_async_copy(
                        ins[part].at[0, :, lanes],
                        held_ref.at[part, :, lanes],
                        in_sems.at[chunk, part],
                    )
                    for part in range(PARTS)
                ]
            )
            for copy in arrivals[-1]:
                copy.start()
        leaving = []
        for dest in range(groups):
            if dest % (groups // chunks) == 0:
                for copy in arrivals[dest // (groups // chunks)]:
                    copy.wait()
            for head in range(heads):
                for part in range(PARTS):
                    start = (dest * heads + head) * width
                    block = held_ref[part, :, start : start + width].astype(jnp.float32)
                    wide_ref[dest % 2, pl.ds(head * PARTS + part, tokens, stride=rows), :] = block
            ready_ref[dest] = (
                wide_ref[dest % 2].reshape(tokens, rows, width).astype(jnp.bfloat16)
            )
            leaving.append(
                pltpu.make_async_copy(ready_ref.at[dest], out_ref.at[dest], out_sems.at[dest])
            )
            leaving[-1].start()
        for copy in leaving:
            copy.wait()

    return pl.pallas_call(
        body,
        out_shape=jax.ShapeDtypeStruct((groups, tokens, rows, width), jnp.bfloat16),
        in_specs=[pl.BlockSpec(memory_space=pl.ANY)] * PARTS,
        out_specs=pl.BlockSpec(memory_space=pl.ANY),
        scratch_shapes=[
            pltpu.VMEM((PARTS, tokens, flat), jnp.bfloat16),
            pltpu.VMEM((groups, tokens, rows, width), jnp.bfloat16),
            pltpu.VMEM((2, tokens * rows, width), jnp.float32),
            pltpu.SemaphoreType.DMA((chunks, PARTS)),
            pltpu.SemaphoreType.DMA((groups,)),
        ],
        compiler_params=pltpu.CompilerParams(vmem_limit_bytes=56 * 2**20),
        cost_estimate=pl.CostEstimate(
            flops=0, bytes_accessed=4 * groups * tokens * rows * width, transcendentals=0
        ),
        name="pack_tokens",
    )(*arrays)


def terms_kernel(
    win_ref,
    order_ref,
    rows_ref,
    gain_q_ref,
    gain_k_ref,
    out_ref,
    wide_ref,
    kv_ref,
    khat_ref,
    qd_ref,
    qe_ref,
    acc_ref,
    *stages,
):
    tiles, count = win_ref.shape
    tokens = tiles * TILE
    heads, width = gain_q_ref.shape
    rows = heads * PARTS
    scale = width ** (-0.5)
    both_refs, ds_refs = stages[:heads], stages[heads:]
    acc_ref[...] = jnp.zeros_like(acc_ref)

    def gather(step, carry):
        for n in range(16):
            place = step * 16 + n
            token = rows_ref[order_ref[place]].astype(jnp.float32)
            wide_ref[pl.ds(pl.multiple_of(place * rows, rows), rows), :] = token
        return carry

    lax.fori_loop(0, tokens // 16, gather, 0)

    def unit_rows(block):
        return block * lax.rsqrt(jnp.mean(block * block, axis=-1, keepdims=True) + 1e-06)

    def arrange(tile, carry):
        for head in range(heads):

            def take(part):
                return wide_ref[
                    pl.ds(tile * TILE * rows + head * PARTS + part, TILE, stride=rows), :
                ]

            qfull = unit_rows(take(0)) * gain_q_ref[head : head + 1, :]
            khat = unit_rows(take(1))
            qn = qfull.astype(jnp.bfloat16)
            kv_ref[head, tile, :, :width] = (khat * gain_k_ref[head : head + 1, :]).astype(
                jnp.bfloat16
            )
            kv_ref[head, tile, :, width:] = take(2).astype(jnp.bfloat16)
            khat_ref[head, tile] = khat
            qd_ref[head, tile, :, :width] = qn
            qd_ref[head, tile, :, width:] = take(3).astype(jnp.bfloat16)
            qe_ref[head, tile] = (qfull - qn.astype(jnp.float32)).astype(jnp.bfloat16)
        return carry

    lax.fori_loop(0, tiles, arrange, 0)
    blank = jnp.zeros((TILE, width), jnp.bfloat16)
    spans = [slice(n * TILE, (n + 1) * TILE) for n in range(count)]

    def fold(block):
        return jnp.sum(block.reshape(-1, 8, width), axis=0)

    def products(head, tile):
        qn, grad = qd_ref[head, tile, :, :width], qd_ref[head, tile, :, width:]
        both_refs[head][...] = lax.dot_general(
            jnp.concatenate([kv_ref[head, win_ref[tile, n]] for n in range(count)], axis=0),
            jnp.concatenate(
                [
                    jnp.concatenate([qn, blank], axis=1),
                    jnp.concatenate([blank, grad], axis=1),
                ],
                axis=0,
            ),
            (((1,), (1,)), ((), ())),
            preferred_element_type=jnp.float32,
        )

    def softmax_grad(head):
        both_ref, ds_ref = both_refs[head], ds_refs[head]
        tops, sums = [], []
        for span in spans:
            scores = both_ref[span, :TILE]
            top = jnp.max(scores, axis=0, keepdims=True)
            weights = jnp.exp2((scores - top) * (scale * LOG2E))
            both_ref[span, :TILE] = weights
            tops.append(top)
            sums.append(jnp.sum(weights, axis=0, keepdims=True))
        highest = tops[0]
        for top in tops[1:]:
            highest = jnp.maximum(highest, top)
        factors = [jnp.exp2((top - highest) * (scale * LOG2E)) for top in tops]
        total = sums[0] * factors[0]
        for n in range(1, count):
            total = total + sums[n] * factors[n]
        inverse = 1.0 / total
        factors = [factor * inverse for factor in factors]
        rowterm = jnp.zeros((8, TILE), jnp.float32)
        for span, factor in zip(spans, factors):
            rounded = (both_ref[span, :TILE] * factor).astype(jnp.bfloat16).astype(jnp.float32)
            rowterm = rowterm + fold(rounded * both_ref[span, TILE:])
        rowterm = jnp.sum(rowterm, axis=0, keepdims=True)
        for span, factor in zip(spans, factors):
            probs = both_ref[span, :TILE] * factor
            ds_ref[span, :] = (probs * (both_ref[span, TILE:] - rowterm)).astype(jnp.bfloat16)

    def key_terms(head, tile):
        sent = jnp.dot(
            ds_refs[head][...],
            jnp.concatenate([qd_ref[head, tile, :, :width], qe_ref[head, tile]], axis=1),
            preferred_element_type=jnp.float32,
        )
        sum_q, sum_k = acc_ref[0, head], acc_ref[1, head]
        for n, span in enumerate(spans):
            pick = win_ref[tile, n]
            dkey, rest = sent[span, :width], sent[span, width:]
            kn = kv_ref[head, pick, :, :width].astype(jnp.float32)
            sum_q = sum_q + fold(kn * (dkey + rest))
            sum_k = sum_k + fold(khat_ref[head, pick] * dkey)
        acc_ref[0, head] = sum_q
        acc_ref[1, head] = sum_k

    last = heads - 1
    for ds_ref in ds_refs:
        ds_ref[...] = jnp.zeros_like(ds_ref)
    products(0, 0)

    def attend(tile, carry):
        for head in range(heads):
            if head < last:
                products(head + 1, tile)
            else:
                products(0, jnp.minimum(tile + 1, tiles - 1))
            softmax_grad(head)
            if head > 0:
                key_terms(head - 1, tile)
            else:
                key_terms(last, jnp.maximum(tile - 1, 0))
        return carry

    lax.fori_loop(0, tiles, attend, 0)
    key_terms(last, tiles - 1)
    for head in range(heads):
        row = slice(head, head + 1)
        sums_q = jnp.sum(acc_ref[0, head], axis=0, keepdims=True)
        sums_k = jnp.sum(acc_ref[1, head], axis=0, keepdims=True)
        out_ref[0, row, :] = sums_q * scale / gain_q_ref[row, :]
        out_ref[1, row, :] = sums_k * scale


def head_terms(rows, order, gain_q, gain_k, windows):
    tokens = rows.shape[0]
    tiles, count = windows.shape
    heads, width = gain_q.shape
    vmem = pl.BlockSpec(memory_space=pltpu.VMEM)
    smem = pl.BlockSpec(memory_space=pltpu.SMEM)
    return pl.pallas_call(
        terms_kernel,
        out_shape=jax.ShapeDtypeStruct((2, heads, width), jnp.float32),
        in_specs=[smem, smem, vmem, vmem, vmem],
        out_specs=vmem,
        scratch_shapes=[
            pltpu.VMEM((tokens * heads * PARTS, width), jnp.float32),
            pltpu.VMEM((heads, tiles, TILE, 2 * width), jnp.bfloat16),
            pltpu.VMEM((heads, tiles, TILE, width), jnp.float32),
            pltpu.VMEM((heads, tiles, TILE, 2 * width), jnp.bfloat16),
            pltpu.VMEM((heads, tiles, TILE, width), jnp.bfloat16),
            pltpu.VMEM((2, heads, 8, width), jnp.float32),
            *[pltpu.VMEM((count * TILE, 2 * TILE), jnp.float32)] * heads,
            *[pltpu.VMEM((count * TILE, TILE), jnp.bfloat16)] * heads,
        ],
        compiler_params=pltpu.CompilerParams(vmem_limit_bytes=28 * 2**20),
        cost_estimate=pl.CostEstimate(
            flops=heads * 10 * tokens * count * TILE * width,
            bytes_accessed=rows.size * 2,
            transcendentals=heads * tokens * count * TILE,
        ),
        name="head_terms",
    )(windows, order, rows, gain_q, gain_k)


def shards(query, key, value, cotangent, gain_q, gain_k, windows, order):
    groups = lax.axis_size("sp")
    spread = lax.axis_size("fsdp")
    tokens = query.shape[1]
    heads, own = gain_q.shape
    width = own * spread

    shares = jnp.stack([gain_q, gain_k]).reshape(1, 2 * heads * own)
    shares = jnp.broadcast_to(shares, (spread, 2 * heads * own))
    shares = lax.all_to_all(shares, "fsdp", split_axis=0, concat_axis=0, tiled=True)
    gains = jnp.transpose(shares.reshape(spread, 2, heads, own), (1, 2, 0, 3))
    gains = gains.reshape(2, heads, width)

    packed = pack((query, key, value, cotangent), groups, heads, width)
    packed, gains = lax.optimization_barrier((packed, gains))
    rows = lax.all_to_all(packed, "sp", split_axis=0, concat_axis=0, tiled=True)
    rows = rows.reshape(groups * tokens, heads * PARTS, width)
    terms = head_terms(rows, order, gains[0], gains[1], windows)
    terms = jnp.transpose(terms.reshape(2, heads, spread, own), (2, 0, 1, 3))
    terms = terms.reshape(spread, 2 * heads * own)
    arrived = lax.all_to_all(terms, "fsdp", split_axis=0, concat_axis=0, tiled=True)
    sums = jnp.sum(arrived, axis=0).reshape(2, heads, own)
    return (sums[0], sums[1])


def solution(mesh):
    placed = (
        P("fsdp", "sp", None),
        P("fsdp", "sp", None),
        P("fsdp", "sp", None),
        P("fsdp", "sp", None),
        P("sp", "fsdp"),
        P("sp", "fsdp"),
        P(),
        P(),
    )
    return jax.shard_map(
        shards,
        mesh=mesh,
        in_specs=placed,
        out_specs=(P("sp", "fsdp"), P("sp", "fsdp")),
        check_vma=False,
    )
```

```python
import jax
import jax.numpy as jnp
from jax import lax
from jax.experimental import pallas as pl
from jax.experimental.pallas import tpu as pltpu
from jax.sharding import PartitionSpec as P

TILE = 128
LOG2E = 1.4426950408889634
PARTS = 4


def pack(arrays, groups, heads, width):
    tokens, flat = arrays[0].shape[1:]
    rows = heads * PARTS
    chunks = 4
    span = flat // chunks

    def body(*refs):
        ins, out_ref = refs[:PARTS], refs[PARTS]
        held_ref, ready_ref, wide_ref, in_sems, out_sems = refs[PARTS + 1 :]
        arrivals = []
        for chunk in range(chunks):
            lanes = slice(chunk * span, (chunk + 1) * span)
            arrivals.append(
                [
                    pltpu.make_async_copy(
                        ins[part].at[0, :, lanes],
                        held_ref.at[part, :, lanes],
                        in_sems.at[chunk, part],
                    )
                    for part in range(PARTS)
                ]
            )
            for copy in arrivals[-1]:
                copy.start()
        leaving = []
        for dest in range(groups):
            if dest % (groups // chunks) == 0:
                for copy in arrivals[dest // (groups // chunks)]:
                    copy.wait()
            for head in range(heads):
                for part in range(PARTS):
                    start = (dest * heads + head) * width
                    block = held_ref[part, :, start : start + width].astype(jnp.float32)
                    wide_ref[dest % 2, pl.ds(head * PARTS + part, tokens, stride=rows), :] = block
            ready_ref[dest] = (
                wide_ref[dest % 2].reshape(tokens, rows, width).astype(jnp.bfloat16)
            )
            leaving.append(
                pltpu.make_async_copy(ready_ref.at[dest], out_ref.at[dest], out_sems.at[dest])
            )
            leaving[-1].start()
        for copy in leaving:
            copy.wait()

    return pl.pallas_call(
        body,
        out_shape=jax.ShapeDtypeStruct((groups, tokens, rows, width), jnp.bfloat16),
        in_specs=[pl.BlockSpec(memory_space=pl.ANY)] * PARTS,
        out_specs=pl.BlockSpec(memory_space=pl.ANY),
        scratch_shapes=[
            pltpu.VMEM((PARTS, tokens, flat), jnp.bfloat16),
            pltpu.VMEM((groups, tokens, rows, width), jnp.bfloat16),
            pltpu.VMEM((2, tokens * rows, width), jnp.float32),
            pltpu.SemaphoreType.DMA((chunks, PARTS)),
            pltpu.SemaphoreType.DMA((groups,)),
        ],
        compiler_params=pltpu.CompilerParams(vmem_limit_bytes=56 * 2**20),
        cost_estimate=pl.CostEstimate(
            flops=0, bytes_accessed=4 * groups * tokens * rows * width, transcendentals=0
        ),
        name="pack_tokens",
    )(*arrays)


def terms_kernel(
    win_ref,
    order_ref,
    rows_ref,
    gain_q_ref,
    gain_k_ref,
    out_ref,
    even_ref,
    odd_ref,
    kv_ref,
    kt_ref,
    qhat_ref,
    qd_ref,
    acc_ref,
    *stages,
):
    tiles, count = win_ref.shape
    tokens = tiles * TILE
    heads, width = gain_q_ref.shape
    rows = heads * PARTS
    scale = width ** (-0.5)
    both_refs, ds_refs = stages[:heads], stages[heads:]
    acc_ref[...] = jnp.zeros_like(acc_ref)

    def gather(tile, wide_ref):
        for n in range(TILE):
            token = rows_ref[order_ref[tile * TILE + n]].astype(jnp.float32)
            wide_ref[n * rows : (n + 1) * rows, :] = token

    def unit_rows(block):
        return block * lax.rsqrt(jnp.mean(block * block, axis=-1, keepdims=True) + 1e-06)

    def split(block):
        rounded = block.astype(jnp.bfloat16)
        return rounded, (block - rounded.astype(jnp.float32)).astype(jnp.bfloat16)

    def arrange(tile, wide_ref):
        for head in range(heads):

            def take(part):
                return wide_ref[pl.ds(head * PARTS + part, TILE, stride=rows), :]

            qhat = unit_rows(take(0))
            kn, rest = split(unit_rows(take(1)) * gain_k_ref[head : head + 1, :])
            kv_ref[head, tile, :, :width] = kn
            kv_ref[head, tile, :, width:] = take(2).astype(jnp.bfloat16)
            kt_ref[head, tile, :width] = kn.T
            kt_ref[head, tile, width:] = rest.T
            qhat_ref[head, tile] = qhat
            qd_ref[head, tile, :, :width] = (qhat * gain_q_ref[head : head + 1, :]).astype(
                jnp.bfloat16
            )
            qd_ref[head, tile, :, width:] = take(3).astype(jnp.bfloat16)

    def in_order(step, carry):
        tile = 2 * step
        gather(tile + 1, odd_ref)
        arrange(tile, even_ref)
        gather(jnp.minimum(tile + 2, tiles - 1), even_ref)
        arrange(tile + 1, odd_ref)
        return carry

    gather(0, even_ref)
    lax.fori_loop(0, tiles // 2, in_order, 0, unroll=2)
    blank = jnp.zeros((TILE, width), jnp.bfloat16)
    spans = [slice(n * TILE, (n + 1) * TILE) for n in range(count)]

    def fold(block):
        return jnp.sum(block.reshape(-1, 8, width), axis=0)

    def products(head, tile):
        qn, grad = qd_ref[head, tile, :, :width], qd_ref[head, tile, :, width:]
        both_refs[head][...] = lax.dot_general(
            jnp.concatenate([kv_ref[head, win_ref[tile, n]] for n in range(count)], axis=0),
            jnp.concatenate(
                [
                    jnp.concatenate([qn, blank], axis=1),
                    jnp.concatenate([blank, grad], axis=1),
                ],
                axis=0,
            ),
            (((1,), (1,)), ((), ())),
            preferred_element_type=jnp.float32,
        )

    def softmax_grad(head):
        both_ref, ds_ref = both_refs[head], ds_refs[head]
        tops, sums = [], []
        for span in spans:
            scores = both_ref[span, :TILE]
            top = jnp.max(scores, axis=0, keepdims=True)
            weights = jnp.exp2((scores - top) * (scale * LOG2E))
            both_ref[span, :TILE] = weights
            tops.append(top)
            sums.append(jnp.sum(weights, axis=0, keepdims=True))
        highest = tops[0]
        for top in tops[1:]:
            highest = jnp.maximum(highest, top)
        factors = [jnp.exp2((top - highest) * (scale * LOG2E)) for top in tops]
        total = sums[0] * factors[0]
        for n in range(1, count):
            total = total + sums[n] * factors[n]
        inverse = 1.0 / total
        factors = [factor * inverse for factor in factors]
        rowterm = jnp.zeros((8, TILE), jnp.float32)
        for span, factor in zip(spans, factors):
            probs = both_ref[span, :TILE] * factor
            both_ref[span, :TILE] = probs
            rounded = probs.astype(jnp.bfloat16).astype(jnp.float32)
            rowterm = rowterm + fold(rounded * both_ref[span, TILE:])
        rowterm = jnp.sum(rowterm, axis=0, keepdims=True)
        for span in spans:
            dscore = both_ref[span, :TILE] * (both_ref[span, TILE:] - rowterm)
            ds_ref[span, :] = dscore.astype(jnp.bfloat16)

    def query_terms(head, tile):
        keys = [kt_ref[head, win_ref[tile, n]] for n in range(count)]
        sent = jnp.dot(
            jnp.concatenate(keys, axis=1), ds_refs[head][...], preferred_element_type=jnp.float32
        )
        dqn, rest = sent[:width].T, sent[width:].T
        acc_ref[0, head] += fold(dqn * qhat_ref[head, tile])
        acc_ref[1, head] += fold((dqn + rest) * qd_ref[head, tile, :, :width].astype(jnp.float32))

    last = heads - 1
    for ds_ref in ds_refs:
        ds_ref[...] = jnp.zeros_like(ds_ref)
    products(0, 0)

    def attend(tile, carry):
        for head in range(heads):
            softmax_grad(head)
            if head < last:
                products(head + 1, tile)
            else:
                products(0, jnp.minimum(tile + 1, tiles - 1))
            if head > 0:
                query_terms(head - 1, tile)
            else:
                query_terms(last, jnp.maximum(tile - 1, 0))
        return carry

    lax.fori_loop(0, tiles, attend, 0, unroll=2)
    query_terms(last, tiles - 1)
    for head in range(heads):
        row = slice(head, head + 1)
        sums_q = jnp.sum(acc_ref[0, head], axis=0, keepdims=True)
        sums_k = jnp.sum(acc_ref[1, head], axis=0, keepdims=True)
        out_ref[0, row, :] = sums_q * scale
        out_ref[1, row, :] = sums_k * scale / gain_k_ref[row, :]


def head_terms(rows, order, gain_q, gain_k, windows):
    tokens = rows.shape[0]
    tiles, count = windows.shape
    heads, width = gain_q.shape
    vmem = pl.BlockSpec(memory_space=pltpu.VMEM)
    smem = pl.BlockSpec(memory_space=pltpu.SMEM)
    return pl.pallas_call(
        terms_kernel,
        out_shape=jax.ShapeDtypeStruct((2, heads, width), jnp.float32),
        in_specs=[smem, smem, vmem, vmem, vmem],
        out_specs=vmem,
        scratch_shapes=[
            pltpu.VMEM((TILE * heads * PARTS, width), jnp.float32),
            pltpu.VMEM((TILE * heads * PARTS, width), jnp.float32),
            pltpu.VMEM((heads, tiles, TILE, 2 * width), jnp.bfloat16),
            pltpu.VMEM((heads, tiles, 2 * width, TILE), jnp.bfloat16),
            pltpu.VMEM((heads, tiles, TILE, width), jnp.float32),
            pltpu.VMEM((heads, tiles, TILE, 2 * width), jnp.bfloat16),
            pltpu.VMEM((2, heads, 8, width), jnp.float32),
            *[pltpu.VMEM((count * TILE, 2 * TILE), jnp.float32)] * heads,
            *[pltpu.VMEM((count * TILE, TILE), jnp.bfloat16)] * heads,
        ],
        compiler_params=pltpu.CompilerParams(vmem_limit_bytes=28 * 2**20),
        cost_estimate=pl.CostEstimate(
            flops=heads * 10 * tokens * count * TILE * width,
            bytes_accessed=rows.size * 2,
            transcendentals=heads * tokens * count * TILE,
        ),
        name="head_terms",
    )(windows, order, rows, gain_q, gain_k)


def shards(query, key, value, cotangent, gain_q, gain_k, windows, order):
    groups = lax.axis_size("sp")
    spread = lax.axis_size("fsdp")
    tokens = query.shape[1]
    heads, own = gain_q.shape
    width = own * spread

    packed = pack((query, key, value, cotangent), groups, heads, width)
    packed, gain_q, gain_k = lax.optimization_barrier((packed, gain_q, gain_k))
    rows = lax.all_to_all(packed, "sp", split_axis=0, concat_axis=0, tiled=True)
    gains = gather_gains(jnp.stack([gain_q, gain_k]), spread)
    rows = rows.reshape(groups * tokens, heads * PARTS, width)
    terms = head_terms(rows, order, gains[0], gains[1], windows)
    terms = jnp.transpose(terms.reshape(2, heads, spread, own), (2, 0, 1, 3))
    terms = terms.reshape(spread, 2 * heads * own)
    arrived = lax.all_to_all(terms, "fsdp", split_axis=0, concat_axis=0, tiled=True)
    sums = jnp.sum(arrived, axis=0).reshape(2, heads, own)
    return (sums[0], sums[1])


def gather_gains(share, spread):
    def from_offset(block, offset):
        return lax.ppermute(block, "fsdp", [(i, i ^ offset) for i in range(spread)])

    shares, offsets = share[None], [0]
    for step in ((1,), (8,), (16,), (2, 4, 6)):
        step = [offset for offset in step if offset < spread]
        parts = [shares] + [from_offset(shares, offset) for offset in step]
        offsets = [own ^ offset for offset in [0] + step for own in offsets]
        shares = jnp.concatenate(parts, axis=0)
    places = jnp.arange(spread, dtype=jnp.int32)[:, None] ^ lax.axis_index("fsdp")
    onehot = (places == jnp.array(offsets, jnp.int32)[None, :]).astype(jnp.float32)
    kinds, heads, own = share.shape
    picked = jnp.sum(onehot[:, :, None] * shares.reshape(1, spread, kinds * heads * own), axis=1)
    gains = jnp.transpose(picked.reshape(spread, kinds, heads, own), (1, 2, 0, 3))
    return gains.reshape(kinds, heads, spread * own)


def solution(mesh):
    placed = (
        P("fsdp", "sp", None),
        P("fsdp", "sp", None),
        P("fsdp", "sp", None),
        P("fsdp", "sp", None),
        P("sp", "fsdp"),
        P("sp", "fsdp"),
        P(),
        P(),
    )
    return jax.shard_map(
        shards,
        mesh=mesh,
        in_specs=placed,
        out_specs=(P("sp", "fsdp"), P("sp", "fsdp")),
        check_vma=False,
    )
```

```python
import functools

import jax
import jax.numpy as jnp
from jax import lax
from jax.experimental import pallas as pl
from jax.experimental.pallas import tpu as pltpu
from jax.sharding import PartitionSpec as P

TILE = 128
LOG2E = 1.4426950408889634
PARTS = 4
INNER = 4


def pack(arrays, head, groups, heads, width, axis=None):
    tokens, flat = arrays[0].shape[1:]
    rows = tokens * PARTS
    chunks = 4
    span = flat // chunks

    def body(*refs):
        ins, out_ref = refs[:PARTS], refs[PARTS]
        held_ref, ready_ref, wide_ref, in_sems, out_sems = refs[PARTS + 1 :]
        arrivals = []
        for chunk in range(chunks):
            lanes = slice(chunk * span, (chunk + 1) * span)
            arrivals.append(
                [
                    pltpu.make_async_copy(
                        ins[part].at[0, :, lanes],
                        held_ref.at[part, :, lanes],
                        in_sems.at[chunk, part],
                    )
                    for part in range(PARTS)
                ]
            )
            for copy in arrivals[-1]:
                copy.start()
        leaving = []
        for dest in range(groups):
            if dest % (groups // chunks) == 0:
                for copy in arrivals[dest // (groups // chunks)]:
                    copy.wait()
            start = (dest * heads + head) * width
            for part in range(PARTS):
                block = held_ref[part, :, start : start + width].astype(jnp.float32)
                wide_ref[dest % 2, pl.ds(part, tokens, stride=PARTS), :] = block
            ready_ref[dest] = wide_ref[dest % 2].astype(jnp.bfloat16)
            place = dest if axis is None else dest ^ lax.axis_index(axis)
            leaving.append(
                pltpu.make_async_copy(ready_ref.at[dest], out_ref.at[place], out_sems.at[dest])
            )
            leaving[-1].start()
        for copy in leaving:
            copy.wait()

    return pl.pallas_call(
        body,
        out_shape=jax.ShapeDtypeStruct((groups, rows, width), jnp.bfloat16),
        in_specs=[pl.BlockSpec(memory_space=pl.ANY)] * PARTS,
        out_specs=pl.BlockSpec(memory_space=pl.ANY),
        scratch_shapes=[
            pltpu.VMEM((PARTS, tokens, flat), jnp.bfloat16),
            pltpu.VMEM((groups, rows, width), jnp.bfloat16),
            pltpu.VMEM((2, rows, width), jnp.float32),
            pltpu.SemaphoreType.DMA((chunks, PARTS)),
            pltpu.SemaphoreType.DMA((groups,)),
        ],
        compiler_params=pltpu.CompilerParams(vmem_limit_bytes=56 * 2**20),
        cost_estimate=pl.CostEstimate(
            flops=0, bytes_accessed=6 * groups * rows * width, transcendentals=0
        ),
        name="pack_head",
    )(*arrays)


def terms_kernel(head, inputs, win_ref, starts_ref, *refs):
    row_refs, (gain_q_ref, gain_k_ref, out_ref) = refs[:inputs], refs[inputs : inputs + 3]
    held_ref, sems, plain_ref, even_ref, odd_ref = refs[inputs + 3 : inputs + 8]
    kv_ref, kt_ref, qhat_ref, qd_ref, acc_ref = refs[inputs + 8 : inputs + 13]
    both_refs, ds_refs = refs[inputs + 13 : inputs + 15], refs[inputs + 15 :]
    tiles, count = win_ref.shape
    width = gain_q_ref.shape[1]
    scale = width ** (-0.5)
    blocks = held_ref.shape[0]
    rows = held_ref.shape[1]
    pieces = sems.shape[0]
    gain_q, gain_k = gain_q_ref[head : head + 1, :], gain_k_ref[head : head + 1, :]

    each = blocks // pieces
    copies = []
    for piece in range(pieces):
        ref = row_refs[piece * inputs // pieces]
        first = piece * each % ref.shape[0]
        copies.append(
            pltpu.make_async_copy(
                ref.at[first : first + each],
                held_ref.at[piece * each : (piece + 1) * each],
                sems.at[piece],
            )
        )
        copies[-1].start()
    acc_ref[...] = jnp.zeros_like(acc_ref)
    for ds_ref in ds_refs:
        ds_ref[...] = jnp.zeros_like(ds_ref)
    for piece in range(pieces):
        copies[piece].wait()
        for block in range(piece * each, (piece + 1) * each):
            plain_ref[block * rows : (block + 1) * rows, :] = held_ref[block].astype(jnp.float32)

    def gather(tile, wide_ref):
        for n in range(TILE):
            start = pl.multiple_of(starts_ref[tile * TILE + n], PARTS)
            wide_ref[n * PARTS : (n + 1) * PARTS, :] = plain_ref[pl.ds(start, PARTS), :]

    def unit_rows(block):
        return block * lax.rsqrt(jnp.mean(block * block, axis=-1, keepdims=True) + 1e-06)

    def split(block):
        rounded = block.astype(jnp.bfloat16)
        return rounded, (block - rounded.astype(jnp.float32)).astype(jnp.bfloat16)

    def arrange(tile, wide_ref):
        def take(part):
            return wide_ref[pl.ds(part, TILE, stride=PARTS), :]

        qhat = unit_rows(take(0))
        kn, rest = split(unit_rows(take(1)) * gain_k)
        kv_ref[tile, :, :width] = kn
        kv_ref[tile, :, width:] = take(2).astype(jnp.bfloat16)
        kt_ref[tile, :width] = kn.T
        kt_ref[tile, width:] = rest.T
        qhat_ref[tile] = qhat
        qd_ref[tile, :, :width] = (qhat * gain_q).astype(jnp.bfloat16)
        qd_ref[tile, :, width:] = take(3).astype(jnp.bfloat16)

    def in_order(step, carry):
        tile = 2 * step
        gather(tile + 1, odd_ref)
        arrange(tile, even_ref)
        gather(jnp.minimum(tile + 2, tiles - 1), even_ref)
        arrange(tile + 1, odd_ref)
        return carry

    gather(0, even_ref)
    lax.fori_loop(0, tiles // 2, in_order, 0, unroll=2)
    blank = jnp.zeros((TILE, width), jnp.bfloat16)
    spans = [slice(n * TILE, (n + 1) * TILE) for n in range(count)]

    def fold(block):
        return jnp.sum(block.reshape(-1, 8, width), axis=0)

    def products(slot, tile):
        qn, grad = qd_ref[tile, :, :width], qd_ref[tile, :, width:]
        both_refs[slot][...] = lax.dot_general(
            jnp.concatenate([kv_ref[win_ref[tile, n]] for n in range(count)], axis=0),
            jnp.concatenate(
                [
                    jnp.concatenate([qn, blank], axis=1),
                    jnp.concatenate([blank, grad], axis=1),
                ],
                axis=0,
            ),
            (((1,), (1,)), ((), ())),
            preferred_element_type=jnp.float32,
        )

    def softmax_grad(slot):
        both_ref, ds_ref = both_refs[slot], ds_refs[slot]
        tops, sums = [], []
        for span in spans:
            scores = both_ref[span, :TILE]
            top = jnp.max(scores, axis=0, keepdims=True)
            weights = jnp.exp2((scores - top) * (scale * LOG2E))
            both_ref[span, :TILE] = weights
            tops.append(top)
            sums.append(jnp.sum(weights, axis=0, keepdims=True))
        highest = tops[0]
        for top in tops[1:]:
            highest = jnp.maximum(highest, top)
        factors = [jnp.exp2((top - highest) * (scale * LOG2E)) for top in tops]
        total = sums[0] * factors[0]
        for n in range(1, count):
            total = total + sums[n] * factors[n]
        inverse = 1.0 / total
        factors = [factor * inverse for factor in factors]
        rowterm = jnp.zeros((8, TILE), jnp.float32)
        for span, factor in zip(spans, factors):
            probs = both_ref[span, :TILE] * factor
            both_ref[span, :TILE] = probs
            rounded = probs.astype(jnp.bfloat16).astype(jnp.float32)
            rowterm = rowterm + fold(rounded * both_ref[span, TILE:])
        rowterm = jnp.sum(rowterm, axis=0, keepdims=True)
        for span in spans:
            dscore = both_ref[span, :TILE] * (both_ref[span, TILE:] - rowterm)
            ds_ref[span, :] = dscore.astype(jnp.bfloat16)

    def query_terms(slot, tile):
        keys = [kt_ref[win_ref[tile, n]] for n in range(count)]
        sent = jnp.dot(
            jnp.concatenate(keys, axis=1), ds_refs[slot][...], preferred_element_type=jnp.float32
        )
        dqn, rest = sent[:width].T, sent[width:].T
        acc_ref[0] += fold(dqn * qhat_ref[tile])
        acc_ref[1] += fold((dqn + rest) * qd_ref[tile, :, :width].astype(jnp.float32))

    products(0, 0)

    def attend(step, carry):
        for slot in range(2):
            tile = 2 * step + slot
            softmax_grad(slot)
            products(1 - slot, jnp.minimum(tile + 1, tiles - 1))
            query_terms(1 - slot, jnp.maximum(tile - 1, 0))
        return carry

    lax.fori_loop(0, tiles // 2, attend, 0, unroll=2)
    query_terms(1, tiles - 1)
    out_ref[0:1, :] = jnp.sum(acc_ref[0], axis=0, keepdims=True) * scale
    out_ref[1:2, :] = jnp.sum(acc_ref[1], axis=0, keepdims=True) * scale / gain_k


def head_terms(rows, starts, gain_q, gain_k, windows, head):
    tiles, count = windows.shape
    width = gain_q.shape[1]
    depth = rows[0].shape[1]
    blocks = sum(block.shape[0] for block in rows)
    tokens = tiles * TILE
    vmem = pl.BlockSpec(memory_space=pltpu.VMEM)
    smem = pl.BlockSpec(memory_space=pltpu.SMEM)
    anywhere = pl.BlockSpec(memory_space=pl.ANY)
    return pl.pallas_call(
        functools.partial(terms_kernel, head, len(rows)),
        out_shape=jax.ShapeDtypeStruct((2, width), jnp.float32),
        in_specs=[smem, smem] + [anywhere] * len(rows) + [vmem, vmem],
        out_specs=vmem,
        scratch_shapes=[
            pltpu.VMEM((blocks, depth, width), jnp.bfloat16),
            pltpu.SemaphoreType.DMA((4,)),
            pltpu.VMEM((blocks * depth, width), jnp.float32),
            pltpu.VMEM((TILE * PARTS, width), jnp.float32),
            pltpu.VMEM((TILE * PARTS, width), jnp.float32),
            pltpu.VMEM((tiles, TILE, 2 * width), jnp.bfloat16),
            pltpu.VMEM((tiles, 2 * width, TILE), jnp.bfloat16),
            pltpu.VMEM((tiles, TILE, width), jnp.float32),
            pltpu.VMEM((tiles, TILE, 2 * width), jnp.bfloat16),
            pltpu.VMEM((2, 8, width), jnp.float32),
            *[pltpu.VMEM((count * TILE, 2 * TILE), jnp.float32)] * 2,
            *[pltpu.VMEM((count * TILE, TILE), jnp.bfloat16)] * 2,
        ],
        compiler_params=pltpu.CompilerParams(vmem_limit_bytes=28 * 2**20),
        cost_estimate=pl.CostEstimate(
            flops=10 * tokens * count * TILE * width,
            bytes_accessed=blocks * depth * width * 2,
            transcendentals=tokens * count * TILE,
        ),
        name="head_terms",
    )(windows, starts, *rows, gain_q, gain_k)


def shards(query, key, value, cotangent, gain_q, gain_k, windows, order):
    groups = lax.axis_size("sp")
    spread = lax.axis_size("fsdp")
    tokens = query.shape[1]
    heads, own = gain_q.shape
    width = own * spread

    arrays = (query, key, value, cotangent)
    first = pack(arrays, 0, groups, heads, width)
    first, gain_q, gain_k, *arrays = lax.optimization_barrier((first, gain_q, gain_k, *arrays))
    first = lax.all_to_all(first, "sp", split_axis=0, concat_axis=0, tiled=True)
    shares, offsets = gather_shares(jnp.stack([gain_q, gain_k])[None], [0], ((1,), (8,), (16,)))
    second = along_y(pack(arrays, 1, groups, heads, width, "sp"))
    shares, *second = lax.optimization_barrier((shares, *second))
    shares, offsets = gather_shares(shares, offsets, ((2, 4, 6),))
    gains = in_channel_order(shares, jnp.array(offsets, jnp.int32), spread)
    second, starts = along_z(second, order, tokens)
    terms = [head_terms([first], order * PARTS, gains[0], gains[1], windows, 0)]
    starts, terms[0] = lax.optimization_barrier((starts, terms[0]))
    terms.append(head_terms(second, starts, gains[0], gains[1], windows, 1))
    terms = jnp.transpose(jnp.stack(terms).reshape(heads, 2, spread, own), (2, 1, 0, 3))
    terms = terms.reshape(spread, 2 * heads * own)
    arrived = lax.all_to_all(terms, "fsdp", split_axis=0, concat_axis=0, tiled=True)
    sums = jnp.sum(arrived, axis=0).reshape(2, heads, own)
    return (sums[0], sums[1])


def permute(block, axis, offset):
    pairs = [(i, i ^ offset) for i in range(lax.axis_size(axis))]
    return lax.ppermute(block, axis, pairs)


def along_y(packed):
    columns = [packed[:INNER]]
    for offset in range(INNER, packed.shape[0], INNER):
        columns.append(permute(packed[offset : offset + INNER], "sp", offset))
    return [jnp.stack([column[n] for column in columns]) for n in range(INNER)]


def along_z(blocks, order, tokens):
    outer = blocks[0].shape[0]
    blocks = [blocks[0]] + [permute(blocks[n], "sp", n) for n in range(1, INNER)]
    away = (order // tokens) ^ lax.axis_index("sp")
    block = (away % INNER) * outer + away // INNER
    return blocks, (block * tokens + order % tokens) * PARTS


def gather_shares(shares, offsets, steps):
    for step in steps:
        parts = [shares] + [permute(shares, "fsdp", offset) for offset in step]
        offsets = [own ^ offset for offset in [0] + list(step) for own in offsets]
        shares = jnp.concatenate(parts, axis=0)
    return shares, offsets


def in_channel_order(shares, offsets, spread):
    places = jnp.arange(spread, dtype=jnp.int32)[:, None] ^ lax.axis_index("fsdp")
    onehot = (places == offsets[None, :]).astype(jnp.float32)
    kinds, heads, own = shares.shape[1:]
    picked = jnp.sum(onehot[:, :, None] * shares.reshape(1, spread, kinds * heads * own), axis=1)
    gains = jnp.transpose(picked.reshape(spread, kinds, heads, own), (1, 2, 0, 3))
    return gains.reshape(kinds, heads, spread * own)


def solution(mesh):
    placed = (
        P("fsdp", "sp", None),
        P("fsdp", "sp", None),
        P("fsdp", "sp", None),
        P("fsdp", "sp", None),
        P("sp", "fsdp"),
        P("sp", "fsdp"),
        P(),
        P(),
    )
    return jax.shard_map(
        shards,
        mesh=mesh,
        in_specs=placed,
        out_specs=(P("sp", "fsdp"), P("sp", "fsdp")),
        check_vma=False,
    )
```

```python
import functools

import jax
import jax.numpy as jnp
from jax import lax
from jax.experimental import pallas as pl
from jax.experimental.pallas import tpu as pltpu
from jax.sharding import PartitionSpec as P

TILE = 128
LOG2E = 1.4426950408889634
PARTS = 4
INNER = 4


def pack(arrays, head, groups, heads, width, axis=None):
    tokens, flat = arrays[0].shape[1:]
    rows = tokens * PARTS
    chunks = 4
    span = flat // chunks

    def body(*refs):
        ins, out_ref = refs[:PARTS], refs[PARTS]
        held_ref, ready_ref, wide_ref, in_sems, out_sems = refs[PARTS + 1 :]
        arrivals = []
        for chunk in range(chunks):
            lanes = slice(chunk * span, (chunk + 1) * span)
            arrivals.append(
                [
                    pltpu.make_async_copy(
                        ins[part].at[0, :, lanes],
                        held_ref.at[part, :, lanes],
                        in_sems.at[chunk, part],
                    )
                    for part in range(PARTS)
                ]
            )
            for copy in arrivals[-1]:
                copy.start()
        leaving = []
        for dest in range(groups):
            if dest % (groups // chunks) == 0:
                for copy in arrivals[dest // (groups // chunks)]:
                    copy.wait()
            start = (dest * heads + head) * width
            for part in range(PARTS):
                block = held_ref[part, :, start : start + width].astype(jnp.float32)
                wide_ref[dest % 2, pl.ds(part, tokens, stride=PARTS), :] = block
            ready_ref[dest] = wide_ref[dest % 2].astype(jnp.bfloat16)
            place = dest if axis is None else dest ^ lax.axis_index(axis)
            leaving.append(
                pltpu.make_async_copy(ready_ref.at[dest], out_ref.at[place], out_sems.at[dest])
            )
            leaving[-1].start()
        for copy in leaving:
            copy.wait()

    return pl.pallas_call(
        body,
        out_shape=jax.ShapeDtypeStruct((groups, rows, width), jnp.bfloat16),
        in_specs=[pl.BlockSpec(memory_space=pl.ANY)] * PARTS,
        out_specs=pl.BlockSpec(memory_space=pl.ANY),
        scratch_shapes=[
            pltpu.VMEM((PARTS, tokens, flat), jnp.bfloat16),
            pltpu.VMEM((groups, rows, width), jnp.bfloat16),
            pltpu.VMEM((2, rows, width), jnp.float32),
            pltpu.SemaphoreType.DMA((chunks, PARTS)),
            pltpu.SemaphoreType.DMA((groups,)),
        ],
        compiler_params=pltpu.CompilerParams(vmem_limit_bytes=56 * 2**20),
        cost_estimate=pl.CostEstimate(
            flops=0, bytes_accessed=6 * groups * rows * width, transcendentals=0
        ),
        name="pack_head",
    )(*arrays)


def terms_kernel(head, inputs, win_ref, starts_ref, *refs):
    row_refs, (gain_q_ref, gain_k_ref, out_ref) = refs[:inputs], refs[inputs : inputs + 3]
    held_ref, sems, plain_ref, even_ref, odd_ref = refs[inputs + 3 : inputs + 8]
    kv_ref, kt_ref, qhat_ref, qd_ref, acc_ref = refs[inputs + 8 : inputs + 13]
    both_refs, ds_refs = refs[inputs + 13 : inputs + 15], refs[inputs + 15 :]
    tiles, count = win_ref.shape
    width = gain_q_ref.shape[1]
    scale = width ** (-0.5)
    blocks = held_ref.shape[0]
    rows = held_ref.shape[1]
    pieces = sems.shape[0]
    gain_q, gain_k = gain_q_ref[head : head + 1, :], gain_k_ref[head : head + 1, :]

    each = blocks // pieces
    copies = []
    for piece in range(pieces):
        ref = row_refs[piece * inputs // pieces]
        first = piece * each % ref.shape[0]
        copies.append(
            pltpu.make_async_copy(
                ref.at[first : first + each],
                held_ref.at[piece * each : (piece + 1) * each],
                sems.at[piece],
            )
        )
        copies[-1].start()
    acc_ref[...] = jnp.zeros_like(acc_ref)
    for ds_ref in ds_refs:
        ds_ref[...] = jnp.zeros_like(ds_ref)
    for piece in range(pieces):
        copies[piece].wait()
        for block in range(piece * each, (piece + 1) * each):
            plain_ref[block * rows : (block + 1) * rows, :] = held_ref[block].astype(jnp.float32)

    def gather(tile, wide_ref):
        for n in range(TILE):
            start = pl.multiple_of(starts_ref[tile * TILE + n], PARTS)
            wide_ref[n * PARTS : (n + 1) * PARTS, :] = plain_ref[pl.ds(start, PARTS), :]

    def unit_rows(block):
        return block * lax.rsqrt(jnp.mean(block * block, axis=-1, keepdims=True) + 1e-06)

    def split(block):
        rounded = block.astype(jnp.bfloat16)
        return rounded, (block - rounded.astype(jnp.float32)).astype(jnp.bfloat16)

    def arrange(tile, wide_ref):
        def take(part):
            return wide_ref[pl.ds(part, TILE, stride=PARTS), :]

        qhat = unit_rows(take(0))
        kn, rest = split(unit_rows(take(1)) * gain_k)
        kv_ref[tile, :, :width] = kn
        kv_ref[tile, :, width:] = take(2).astype(jnp.bfloat16)
        kt_ref[tile, :width] = kn.T
        kt_ref[tile, width:] = rest.T
        qhat_ref[tile] = qhat
        qd_ref[tile, :, :width] = (qhat * gain_q).astype(jnp.bfloat16)
        qd_ref[tile, :, width:] = take(3).astype(jnp.bfloat16)

    def in_order(step, carry):
        tile = 2 * step
        gather(tile + 1, odd_ref)
        arrange(tile, even_ref)
        gather(jnp.minimum(tile + 2, tiles - 1), even_ref)
        arrange(tile + 1, odd_ref)
        return carry

    gather(0, even_ref)
    lax.fori_loop(0, tiles // 2, in_order, 0, unroll=8)
    blank = jnp.zeros((TILE, width), jnp.bfloat16)
    spans = [slice(n * TILE, (n + 1) * TILE) for n in range(count)]

    def fold(block):
        return jnp.sum(block.reshape(-1, 8, width), axis=0)

    def products(slot, tile):
        qn, grad = qd_ref[tile, :, :width], qd_ref[tile, :, width:]
        both_refs[slot][...] = lax.dot_general(
            jnp.concatenate([kv_ref[win_ref[tile, n]] for n in range(count)], axis=0),
            jnp.concatenate(
                [
                    jnp.concatenate([qn, blank], axis=1),
                    jnp.concatenate([blank, grad], axis=1),
                ],
                axis=0,
            ),
            (((1,), (1,)), ((), ())),
            preferred_element_type=jnp.float32,
        )

    def softmax_grad(slot):
        both_ref, ds_ref = both_refs[slot], ds_refs[slot]
        tops, sums = [], []
        for span in spans:
            scores = both_ref[span, :TILE]
            top = jnp.max(scores, axis=0, keepdims=True)
            weights = jnp.exp2((scores - top) * (scale * LOG2E))
            both_ref[span, :TILE] = weights
            tops.append(top)
            sums.append(jnp.sum(weights, axis=0, keepdims=True))
        highest = tops[0]
        for top in tops[1:]:
            highest = jnp.maximum(highest, top)
        factors = [jnp.exp2((top - highest) * (scale * LOG2E)) for top in tops]
        total = sums[0] * factors[0]
        for n in range(1, count):
            total = total + sums[n] * factors[n]
        inverse = 1.0 / total
        factors = [factor * inverse for factor in factors]
        rowterm = jnp.zeros((8, TILE), jnp.float32)
        for span, factor in zip(spans, factors):
            probs = both_ref[span, :TILE] * factor
            both_ref[span, :TILE] = probs
            rounded = probs.astype(jnp.bfloat16).astype(jnp.float32)
            rowterm = rowterm + fold(rounded * both_ref[span, TILE:])
        rowterm = jnp.sum(rowterm, axis=0, keepdims=True)
        for span in spans:
            dscore = both_ref[span, :TILE] * (both_ref[span, TILE:] - rowterm)
            ds_ref[span, :] = dscore.astype(jnp.bfloat16)

    def query_terms(slot, tile):
        keys = [kt_ref[win_ref[tile, n]] for n in range(count)]
        sent = jnp.dot(
            jnp.concatenate(keys, axis=1), ds_refs[slot][...], preferred_element_type=jnp.float32
        )
        dqn, rest = sent[:width].T, sent[width:].T
        acc_ref[0] += fold(dqn * qhat_ref[tile])
        acc_ref[1] += fold((dqn + rest) * qd_ref[tile, :, :width].astype(jnp.float32))

    products(0, 0)

    def attend(step, carry):
        for slot in range(2):
            tile = 2 * step + slot
            softmax_grad(slot)
            products(1 - slot, jnp.minimum(tile + 1, tiles - 1))
            query_terms(1 - slot, jnp.maximum(tile - 1, 0))
        return carry

    lax.fori_loop(0, tiles // 2, attend, 0, unroll=8)
    query_terms(1, tiles - 1)
    out_ref[0:1, :] = jnp.sum(acc_ref[0], axis=0, keepdims=True) * scale
    out_ref[1:2, :] = jnp.sum(acc_ref[1], axis=0, keepdims=True) * scale / gain_k


def head_terms(rows, starts, gain_q, gain_k, windows, head):
    tiles, count = windows.shape
    width = gain_q.shape[1]
    depth = rows[0].shape[1]
    blocks = sum(block.shape[0] for block in rows)
    tokens = tiles * TILE
    vmem = pl.BlockSpec(memory_space=pltpu.VMEM)
    smem = pl.BlockSpec(memory_space=pltpu.SMEM)
    anywhere = pl.BlockSpec(memory_space=pl.ANY)
    return pl.pallas_call(
        functools.partial(terms_kernel, head, len(rows)),
        out_shape=jax.ShapeDtypeStruct((2, width), jnp.float32),
        in_specs=[smem, smem] + [anywhere] * len(rows) + [vmem, vmem],
        out_specs=vmem,
        scratch_shapes=[
            pltpu.VMEM((blocks, depth, width), jnp.bfloat16),
            pltpu.SemaphoreType.DMA((4,)),
            pltpu.VMEM((blocks * depth, width), jnp.float32),
            pltpu.VMEM((TILE * PARTS, width), jnp.float32),
            pltpu.VMEM((TILE * PARTS, width), jnp.float32),
            pltpu.VMEM((tiles, TILE, 2 * width), jnp.bfloat16),
            pltpu.VMEM((tiles, 2 * width, TILE), jnp.bfloat16),
            pltpu.VMEM((tiles, TILE, width), jnp.float32),
            pltpu.VMEM((tiles, TILE, 2 * width), jnp.bfloat16),
            pltpu.VMEM((2, 8, width), jnp.float32),
            *[pltpu.VMEM((count * TILE, 2 * TILE), jnp.float32)] * 2,
            *[pltpu.VMEM((count * TILE, TILE), jnp.bfloat16)] * 2,
        ],
        compiler_params=pltpu.CompilerParams(vmem_limit_bytes=28 * 2**20),
        cost_estimate=pl.CostEstimate(
            flops=10 * tokens * count * TILE * width,
            bytes_accessed=blocks * depth * width * 2,
            transcendentals=tokens * count * TILE,
        ),
        name="head_terms",
    )(windows, starts, *rows, gain_q, gain_k)


def shards(query, key, value, cotangent, gain_q, gain_k, windows, order):
    groups = lax.axis_size("sp")
    spread = lax.axis_size("fsdp")
    tokens = query.shape[1]
    heads, own = gain_q.shape
    width = own * spread

    arrays = (query, key, value, cotangent)
    first = pack(arrays, 0, groups, heads, width)
    first, gain_q, gain_k, *arrays = lax.optimization_barrier((first, gain_q, gain_k, *arrays))
    first = lax.all_to_all(first, "sp", split_axis=0, concat_axis=0, tiled=True)
    shares, offsets = gather_shares(jnp.stack([gain_q, gain_k])[None], [0], ((1,), (8,), (16,)))
    second = along_y(pack(arrays, 1, groups, heads, width, "sp"))
    shares, *second = lax.optimization_barrier((shares, *second))
    shares, offsets = gather_shares(shares, offsets, ((2, 4, 6),))
    shares, second[2] = lax.optimization_barrier((shares, second[2]))
    gains = in_channel_order(shares, jnp.array(offsets, jnp.int32), spread)
    second, starts = along_z(second, order, tokens)
    terms = [head_terms([first], order * PARTS, gains[0], gains[1], windows, 0)]
    starts, terms[0] = lax.optimization_barrier((starts, terms[0]))
    terms.append(head_terms(second, starts, gains[0], gains[1], windows, 1))
    terms = jnp.transpose(jnp.stack(terms).reshape(heads, 2, spread, own), (2, 1, 0, 3))
    terms = terms.reshape(spread, 2 * heads * own)
    arrived = lax.all_to_all(terms, "fsdp", split_axis=0, concat_axis=0, tiled=True)
    sums = jnp.sum(arrived, axis=0).reshape(2, heads, own)
    return (sums[0], sums[1])


def permute(block, axis, offset):
    pairs = [(i, i ^ offset) for i in range(lax.axis_size(axis))]
    return lax.ppermute(block, axis, pairs)


def along_y(packed):
    columns = [packed[:INNER]]
    for offset in range(INNER, packed.shape[0], INNER):
        columns.append(permute(packed[offset : offset + INNER], "sp", offset))
    return [jnp.stack([column[n] for column in columns]) for n in range(INNER)]


def along_z(blocks, order, tokens):
    outer = blocks[0].shape[0]
    blocks = [blocks[0]] + [permute(blocks[n], "sp", n) for n in range(1, INNER)]
    away = (order // tokens) ^ lax.axis_index("sp")
    block = (away % INNER) * outer + away // INNER
    return blocks, (block * tokens + order % tokens) * PARTS


def gather_shares(shares, offsets, steps):
    for step in steps:
        parts = [shares] + [permute(shares, "fsdp", offset) for offset in step]
        offsets = [own ^ offset for offset in [0] + list(step) for own in offsets]
        shares = jnp.concatenate(parts, axis=0)
    return shares, offsets


def in_channel_order(shares, offsets, spread):
    places = jnp.arange(spread, dtype=jnp.int32)[:, None] ^ lax.axis_index("fsdp")
    onehot = (places == offsets[None, :]).astype(jnp.float32)
    kinds, heads, own = shares.shape[1:]
    picked = jnp.sum(onehot[:, :, None] * shares.reshape(1, spread, kinds * heads * own), axis=1)
    gains = jnp.transpose(picked.reshape(spread, kinds, heads, own), (1, 2, 0, 3))
    return gains.reshape(kinds, heads, spread * own)


def solution(mesh):
    placed = (
        P("fsdp", "sp", None),
        P("fsdp", "sp", None),
        P("fsdp", "sp", None),
        P("fsdp", "sp", None),
        P("sp", "fsdp"),
        P("sp", "fsdp"),
        P(),
        P(),
    )
    return jax.shard_map(
        shards,
        mesh=mesh,
        in_specs=placed,
        out_specs=(P("sp", "fsdp"), P("sp", "fsdp")),
        check_vma=False,
    )
```
